32 devices in a mesh: groups: 2 (over y), cls: 4 (over x, core), proj: 4 (over z).
Axes of the slice: x: 2, y: 2, z: 4, core: 2. Of those that a mesh axis runs over, the one named last changes fastest.
Arguments:
- particles: bfloat16 [512, 4096], P(('groups', 'cls', 'proj')), parts along dimension 0, may hold values from -6 to 6
- classes: int32 [512, 1], P(('groups', 'cls', 'proj')), parts along dimension 0, may hold values from 0 to 3; in each aligned block of 16 rows (0 to 15, 16 to 31, ...) at most 12 rows name the same one
- windows: int32 [512, 2], P(('groups', 'cls', 'proj')), parts along dimension 0, may hold values from -3 to 3
- pose_lists: int32 [512, 8], P(('groups', 'cls', 'proj')), parts along dimension 0, may hold values from 0 to 15, all different within a row
- inverse_noise: bfloat16 [512], P(('groups', 'cls', 'proj')), parts along dimension 0, may hold values from 0.19921875 to 2
- projections: bfloat16 [4, 2048, 4096], P('cls', 'proj'), may hold values from -0.09375 to 0.09375
Outputs:
- posterior: float32 [512, 16, 2048], P(('groups', 'cls', 'proj')), parts along dimension 0
- evidence: float32 [512], P(('groups', 'cls', 'proj')), parts along dimension 0
The draws below stay inside these ranges and needn't reach their ends.
There are 2 independent parts, one for each index of `groups`. The reference program is written for one: setup_inputs(seed, part) draws one part's arguments, and reference() takes and returns one part's arrays. A program takes and returns all parts, laid end to end along the dimension named above; an argument that names none is the same for every part. Nothing has to cross between parts.
Inputs may be any that keep to these rules, and one draw needn't show every extreme that they name: `classes`: within the rows of one device (aligned blocks of 16 rows) no class group is named by more than 12 rows, and in every draw some class group is named by exactly 12 rows of some device. `pose_lists`: each row names 8 different pose blocks.
All inputs are finite; a program needn't handle non-finite values.
Results may differ from the reference program's by a relative error of at most 0.0069.
Values may be sent and summed in bfloat16 or wider, within the bound.
No kernel may reach another device: no remote copies, remote signals or barrier semaphores. Data moves between devices by JAX's collectives and lax.ppermute only.
A program may use at most 128 MiB of HBM per device.

```python
import math
import jax
import jax.numpy as jnp
import numpy as np
from jax import lax

IMG = 64
KF = 2048
J = 2048
NB = 16
NSEL = 8
SW = 4
SH = 16
P_DEV = 16
CAP = 12
CG = 4
PARTICLES = 256
N_CLS = 4


def place_ends(array, rng, low, high):
    longest = array.shape.index(max(array.shape))
    spots = []
    for shift in (0, 1):
        where = [jax.random.randint(jax.random.fold_in(rng, axis), (), 0, length) for axis, length in enumerate(array.shape)]
        where[longest] = (where[longest] + shift) % array.shape[longest]
        spots.append(tuple(where))
    return array.at[spots[0]].set(low).at[spots[1]].set(high)


def level_of(rng, shape, split, smallest, largest):
    loudness = 1.0
    for axis_at, shards_of in split:
        draws = jax.random.uniform(jax.random.fold_in(jax.random.fold_in(rng, 6), axis_at), (shards_of,), jnp.float32, smallest / len(split), largest / len(split))
        loudness = loudness * jnp.repeat(jnp.exp(draws), shape[axis_at] // shards_of).reshape((-1,) + (1,) * (len(shape) - 1 - axis_at))
    return loudness


def picks_of(stream_key, rows, amount, top, lift):
    ranking = jax.random.permutation(jax.random.fold_in(stream_key, 1), amount)
    pull = ranking
    for power in range(3):
        pull = pull * pull // amount
    pull = pull * lift // amount
    chance = jax.random.randint(jax.random.fold_in(stream_key, 2), (rows, amount), 0, 4096) + pull
    sure = jax.random.permutation(jax.random.fold_in(stream_key, 3), rows)[jnp.arange(amount) % rows]
    chance = jnp.where(jnp.arange(rows)[:, None] == sure[None, :], 1 << 14, chance)
    priority = chance * amount + jnp.arange(amount)
    return lax.top_k(priority.astype(jnp.int32), top)[1].astype(jnp.int32)


def deal_out(key, own, number, rows, count, top, limit, lean):
    order = jax.random.permutation(key, count)
    packed, ordinary = portions_of(count, rows * top, limit, lean, True), portions_of(count, rows * top, limit, lean, False)
    places = jnp.arange(count)

    def named(tallies, offset_by):
        used = int((tallies > 0).sum())
        fixed = max(1, used // 4)
        passed = fixed + (places - fixed + offset_by * (used - fixed)) % max(1, count - fixed)
        return jnp.zeros((count,), jnp.int32).at[order[jnp.where(places < fixed, places, passed)]].set(jnp.asarray(tallies, jnp.int32))

    tallies = jnp.where(number % 4 == 0, named(packed, number // 4), named(ordinary, number - number // 4 - 1))
    mixed = jax.random.permutation(jax.random.fold_in(own, 3), count)
    donor, taker = mixed[0:count // 2 * 2:2], mixed[1:count // 2 * 2:2]
    margin = jnp.minimum(tallies[donor] - 1, limit - tallies[taker]) // 2
    margin = jnp.where((donor == order[0]) | (taker == order[0]) | (tallies[taker] == 0), 0, jnp.maximum(margin, 0))
    passed = jax.random.randint(jax.random.fold_in(own, 4), (count // 2,), 0, 1 << 20) % (margin + 1)
    tallies = tallies.at[donor].add(-passed).at[taker].add(passed)
    members = jnp.searchsorted(jnp.cumsum(tallies), jnp.arange(rows * top), side="right").astype(jnp.int32)
    listing = members.reshape(top, rows).T
    listing = listing[jax.random.permutation(jax.random.fold_in(own, 1), rows)]
    offset_by = jax.random.randint(jax.random.fold_in(own, 2), (rows, 1), 0, top)
    return jnp.take_along_axis(listing, (jnp.arange(top)[None, :] + offset_by) % top, axis=1)


def portions_of(number_of, total, bound, lean, full):
    portions = [(1 << 20) // math.isqrt(rank ** lean) + 1 for rank in range(1, number_of + 1)]
    largest = bound if full else min(bound, max(-(-total // number_of), total * portions[0] // sum(portions)))
    least = 1 if total - largest >= number_of - 1 else 0
    holding, spare = [largest] + [least] * (number_of - 1), total - largest - least * (number_of - 1)
    while spare > 0:
        movable = [i for i in range(1, number_of) if holding[i] < largest] or [i for i in range(1, number_of) if holding[i] < bound]
        pool, left = sum([portions[i] for i in movable]), spare
        for i in movable:
            addition = min(bound - holding[i], max(1, left * portions[i] // pool), spare)
            holding[i] = holding[i] + addition
            spare = spare - addition
    return np.array(holding)


def gaussian(own_key, shape, scale, bound, pieces=(), kind=jnp.bfloat16):
    gain = level_of(own_key, shape, pieces, -0.22, 0.18) if pieces else 1.0
    drawn = jax.random.normal(own_key, shape, jnp.float32) * scale * gain
    return jnp.minimum(jnp.maximum(drawn, -bound), bound).astype(kind)


def setup_inputs(seed: int = 0, part: int = 0) -> dict:
    streams_of = jax.random.split(jax.random.key(seed), 7)
    part_splits = jax.random.split(jax.random.fold_in(streams_of[6], part), 7)
    particles = gaussian(part_splits[0], (PARTICLES, 2 * KF), 1.0, 6.0, ((0, 16),))
    classes_keys = jax.random.split(jax.random.fold_in(part_splits[1], 1), PARTICLES // P_DEV)
    classes_turns = jax.random.permutation(jax.random.fold_in(part_splits[1], 3), PARTICLES // P_DEV)
    classes = jax.vmap(lambda own, number: deal_out(jax.random.fold_in(part_splits[1], 2), own, number, P_DEV, N_CLS, 1, CAP, 2))(classes_keys, classes_turns).reshape((PARTICLES, 1))
    windows = place_ends(jax.random.randint(part_splits[2], (PARTICLES, 2), -3, 4), jax.random.fold_in(part_splits[2], 1), -3, 3).astype(jnp.int32)
    pose_lists = picks_of(part_splits[3], PARTICLES, NB, NSEL, 0)
    inverse_noise = jnp.clip(jnp.exp(math.log(2.0) - 2.306499 * jax.random.uniform(part_splits[4], (PARTICLES,), jnp.float32) ** level_of(part_splits[4], (PARTICLES,), ((0, 16),), -0.2, 0.2)), 0.19921875, 2.0).astype(jnp.bfloat16)
    projections = gaussian(streams_of[5], (CG, J, 2 * KF), (2 * KF) ** -0.5, 0.09375, ((0, 4), (1, 4)))
    return dict(particles=particles, classes=classes, windows=windows, pose_lists=pose_lists, inverse_noise=inverse_noise, projections=projections)


def wave_table(half, side):
    indices = jnp.arange(half, dtype=jnp.int32)
    wave_y = (indices // side).astype(jnp.float32)
    wave_x = (indices % side - side // 2).astype(jnp.float32)
    return wave_x, wave_y


def shift_rows(row_block, centre_x, centre_y, side, across):
    half = row_block.shape[1] // 2
    wave_x, wave_y = wave_table(half, side)
    offsets = jnp.arange(across * across, dtype=jnp.int32)
    offset_x = (offsets % across - across // 2).astype(jnp.float32)
    offset_y = (offsets // across - across // 2).astype(jnp.float32)
    moved_x = centre_x[:, None] + offset_x[None, :]
    moved_y = centre_y[:, None] + offset_y[None, :]
    phases = (moved_x[:, :, None] * wave_x + moved_y[:, :, None] * wave_y) * (2.0 * math.pi / side)
    cosine = jnp.cos(phases)
    sine = jnp.sin(phases)
    real_part = row_block[:, None, :half].astype(jnp.float32)
    imag_part = row_block[:, None, half:].astype(jnp.float32)
    new_real = real_part * cosine + imag_part * sine
    new_imag = imag_part * cosine - real_part * sine
    return jnp.concatenate([new_real, new_imag], axis=2).astype(jnp.bfloat16)


def block_mask(chosen, block_count):
    block_labels = jnp.arange(block_count, dtype=jnp.int32)
    return jnp.max((chosen[:, :, None] == block_labels[None, None, :]).astype(jnp.float32), axis=1)


def reference(particles, classes, windows, pose_lists, inverse_noise, projections):
    masks = block_mask(pose_lists, NB)

    def single(inputs):
        image_row, group, window, mask_row, noise_level = inputs
        own_panel = projections[group]
        centres = window.astype(jnp.float32)
        shifted = shift_rows(image_row[None, :], centres[0:1], centres[1:2], IMG, SW)[0]
        scores = jnp.dot(shifted, own_panel.T, preferred_element_type=jnp.float32) * noise_level.astype(jnp.float32)
        allowed = jnp.repeat(mask_row, J // NB)
        terms = jnp.exp(scores) * allowed[None, :]
        mean_term = jnp.sum(terms) / (SH * J)
        return terms / mean_term, jnp.log(mean_term)

    posterior, evidence = lax.map(single, (particles, classes[:, 0], windows, masks, inverse_noise))
    return posterior, evidence
```

```python
import functools
import math

import jax
import jax.numpy as jnp
import numpy as np
from jax import lax
from jax.experimental import pallas as pl
from jax.experimental.pallas import tpu as pltpu
from jax.sharding import PartitionSpec as P

IMG = 64
KF = 2048
J = 2048
NB = 16
SW = 4
SH = 16
LANES = 128
HALVES = 2 * KF // LANES
TILE = 16
BLOCK = J // NB
CHUNKS = 1
BF16_MAX = float(jnp.finfo(jnp.bfloat16).max)


def relative_tables():
    c = np.arange(KF)
    kx, ky = c % IMG - IMG // 2, c // IMG
    s = np.arange(SH)
    turn = (s % SW - SW // 2)[:, None] * kx + (s // SW - SW // 2)[:, None] * ky
    phase = (turn % IMG) * (2.0 * math.pi / IMG)
    return np.cos(phase).astype(np.float32), np.sin(phase).astype(np.float32)


def score_kernel(
    me_ref, rows_ref, own_hbm, other_hbm, cos_ref, sin_ref, out_ref,
    centred, panels, shifted, scores, details, facts, members, panel_sems, fact_sem,
):
    pieces, count, _ = rows_ref.shape
    load = [
        pltpu.make_async_copy(own_hbm, panels.at[0], panel_sems.at[0]),
        pltpu.make_async_copy(other_hbm, panels.at[1], panel_sems.at[1]),
    ]
    load[0].start()
    load[1].start()
    for s in range(pieces):
        details[s * count:(s + 1) * count, :] = rows_ref[s, :, 2 * KF:].astype(jnp.float32)
    send = pltpu.make_async_copy(details, facts, fact_sem)
    send.start()

    lane = lax.broadcasted_iota(jnp.int32, (count, LANES), 1)
    kx = (lane % IMG - IMG // 2).astype(jnp.float32)
    odd = (lane // IMG).astype(jnp.float32)
    unit = 2.0 * math.pi / IMG
    for s in range(pieces):
        fact = details[s * count:(s + 1) * count, :]
        wx = jnp.broadcast_to(fact[:, 1:2], (count, LANES))
        wy = jnp.broadcast_to(fact[:, 2:3], (count, LANES))
        angle = (wx * kx + wy * odd) * unit
        step = wy * (2.0 * unit)
        cosine, sine = jnp.cos(angle), jnp.sin(angle)
        step_cos, step_sin = jnp.cos(step), jnp.sin(step)
        for t in range(KF // LANES):
            at = slice(t * LANES, (t + 1) * LANES)
            to = slice(KF + t * LANES, KF + (t + 1) * LANES)
            re = rows_ref[s, :, at].astype(jnp.float32)
            im = rows_ref[s, :, to].astype(jnp.float32)
            centred[pl.ds(s * count * HALVES + t, count, HALVES), :] = re * cosine + im * sine
            centred[pl.ds(s * count * HALVES + HALVES // 2 + t, count, HALVES), :] = im * cosine - re * sine
            cosine, sine = (
                cosine * step_cos - sine * step_sin,
                sine * step_cos + cosine * step_sin,
            )
    send.wait()

    own = me_ref[0]
    first_block = me_ref[1]

    def sort_row(row, filled):
        label = facts[row, 0].astype(jnp.int32)
        members[0, filled[0]] = row
        members[1, filled[1]] = row
        return (
            filled[0] + (label == own).astype(jnp.int32),
            filled[1] + (label == own + 1 - 2 * (own % 2)).astype(jnp.int32),
        )

    totals = lax.fori_loop(0, pieces * count, sort_row, (jnp.int32(0), jnp.int32(0)))

    for which in range(2):
        load[which].wait()

        @pl.loop(0, (totals[which] + TILE - 1) // TILE)
        def _(tile):
            base = tile * TILE
            present = jnp.minimum(totals[which] - base, TILE)

            @pl.loop(0, present)
            def _(q):
                row = members[which, base + q]
                place = pl.ds(pl.multiple_of(q * SH, SH), SH)
                image = centred[pl.ds(pl.multiple_of(row * HALVES, HALVES), HALVES), :]
                for t in range(KF // LANES):
                    at = slice(t * LANES, (t + 1) * LANES)
                    to = slice(KF + t * LANES, KF + (t + 1) * LANES)
                    re = jnp.broadcast_to(image[t:t + 1, :], (SH, LANES))
                    im = jnp.broadcast_to(image[HALVES // 2 + t:HALVES // 2 + t + 1, :], (SH, LANES))
                    cosine, sine = cos_ref[:, at], sin_ref[:, at]
                    shifted[place, at] = (re * cosine + im * sine).astype(jnp.bfloat16)
                    shifted[place, to] = (im * cosine - re * sine).astype(jnp.bfloat16)

            scores[...] = lax.dot_general(
                shifted[...], panels[which], (((1,), (1,)), ((), ())),
                preferred_element_type=jnp.float32,
            )

            @pl.loop(0, present)
            def _(q):
                row = members[which, base + q]
                noise = facts[row, 3]
                place = pl.ds(pl.multiple_of(q * SH, SH), SH)
                for b in range(out_ref.shape[3] // BLOCK):
                    at = slice(b * BLOCK, (b + 1) * BLOCK)
                    allowed = facts[row, 4 + first_block + b]
                    term = jnp.minimum(jnp.exp(scores[place, at] * noise), BF16_MAX)
                    out_ref[row // count, row % count, :, at] = (term * allowed).astype(jnp.bfloat16)


def score(me, rows, own_panel, other_panel, cosine, sine):
    pieces, count, _ = rows.shape
    depth = own_panel.shape[0]
    total = pieces * count
    return pl.pallas_call(
        score_kernel,
        out_shape=jax.ShapeDtypeStruct((pieces, count, SH, depth), jnp.bfloat16),
        in_specs=[
            pl.BlockSpec(memory_space=pltpu.SMEM),
            pl.BlockSpec(memory_space=pltpu.VMEM),
            pl.BlockSpec(memory_space=pl.ANY),
            pl.BlockSpec(memory_space=pl.ANY),
            pl.BlockSpec(memory_space=pltpu.VMEM),
            pl.BlockSpec(memory_space=pltpu.VMEM),
        ],
        out_specs=pl.BlockSpec(memory_space=pltpu.VMEM),
        scratch_shapes=[
            pltpu.VMEM((total * HALVES, LANES), jnp.float32),
            pltpu.VMEM((2, depth, 2 * KF), jnp.bfloat16),
            pltpu.VMEM((TILE * SH, 2 * KF), jnp.bfloat16),
            pltpu.VMEM((TILE * SH, depth), jnp.float32),
            pltpu.VMEM((total, LANES), jnp.float32),
            pltpu.SMEM((total, LANES), jnp.float32),
            pltpu.SMEM((2, total + TILE), jnp.int32),
            pltpu.SemaphoreType.DMA((2,)),
            pltpu.SemaphoreType.DMA,
        ],
        compiler_params=pltpu.CompilerParams(vmem_limit_bytes=48 * 1024 * 1024),
        name="score",
    )(me, rows, own_panel, other_panel, cosine, sine)


def weigh_kernel(places, chunks, me_ref, *refs):
    parts, (weights_ref, log_ref) = refs[:-2], refs[-2:]
    depth = parts[0].shape[-1]
    count = parts[0].shape[0]
    lane = lax.broadcasted_iota(jnp.int32, log_ref.shape, 1)
    logs = jnp.zeros(log_ref.shape, jnp.float32)
    for j in range(chunks):
        def one(p, logs, j=j):
            terms = [parts[j * places + s][p].astype(jnp.float32) for s in range(places)]
            total = sum(terms)
            mean = jnp.sum(total, keepdims=True) / (SH * J)
            for s in range(places):
                at = pl.multiple_of(lax.rem(me_ref[2] + s, places) * depth, depth)
                weights_ref[j * count + p, :, pl.ds(at, depth)] = terms[s] / mean
            return jnp.where(lane == j * count + p, jnp.log(mean), logs)

        logs = lax.fori_loop(0, count, one, logs)
    log_ref[...] = logs


def weigh(me, parts, places, chunks):
    count, _, depth = parts[0].shape
    rows = chunks * count
    return pl.pallas_call(
        functools.partial(weigh_kernel, places, chunks),
        out_shape=(
            jax.ShapeDtypeStruct((rows, SH, J), jnp.float32),
            jax.ShapeDtypeStruct((1, rows), jnp.float32),
        ),
        in_specs=[pl.BlockSpec(memory_space=pltpu.SMEM)]
        + [pl.BlockSpec(memory_space=pltpu.VMEM)] * len(parts),
        out_specs=(
            pl.BlockSpec(memory_space=pltpu.VMEM),
            pl.BlockSpec(memory_space=pltpu.VMEM),
        ),
        compiler_params=pltpu.CompilerParams(vmem_limit_bytes=32 * 1024 * 1024),
        name="weigh",
    )(me, *parts)


def block_mask(chosen):
    labels = jnp.arange(NB, dtype=jnp.int32)
    return jnp.max((chosen[:, :, None] == labels[None, None, :]).astype(jnp.bfloat16), axis=1)


def per_device(particles, classes, windows, pose_lists, inverse_noise, projections):
    owners = lax.axis_size("cls")
    places = lax.axis_size("proj")
    pairs = owners // 2
    label, place = lax.axis_index("cls"), lax.axis_index("proj")
    own_x = label // 2
    depth = projections.shape[1]
    me = jnp.stack([label, place * (depth // BLOCK), place]).astype(jnp.int32)

    def along_x(value, by):
        return lax.ppermute(
            value, "cls", [(i, (i + 2 * by) % owners) for i in range(owners)]
        )

    def along_z(value, by):
        return lax.ppermute(
            value, "proj", [(i, (i + by) % places) for i in range(places)]
        )

    rows = jnp.concatenate(
        [
            particles,
            classes.astype(jnp.bfloat16),
            windows.astype(jnp.bfloat16),
            inverse_noise[:, None],
            block_mask(pose_lists),
            jnp.zeros((particles.shape[0], LANES - NB - 4), jnp.bfloat16),
        ],
        axis=1,
    )
    count = rows.shape[0] // CHUNKS
    cosine, sine = (jnp.asarray(table) for table in relative_tables())
    own_panel = projections[0]
    other_panel = lax.ppermute(own_panel, "cls", [(i, i ^ 1) for i in range(owners)])

    parts = []
    for j in range(CHUNKS):
        mine = rows[j * count:(j + 1) * count]
        column = jnp.stack([mine] + [along_z(mine, s) for s in range(1, places)])
        far = [along_x(column, f) for f in range(1, pairs)]
        far_terms = [
            along_x(score(me, far[f - 1], own_panel, other_panel, cosine, sine), -f)
            for f in range(1, pairs)
        ]
        merged = score(me, column, own_panel, other_panel, cosine, sine)
        owner_x = column[:, :, 2 * KF].astype(jnp.int32) // 2
        for f in range(1, pairs):
            there = owner_x == (own_x + f) % pairs
            merged = jnp.where(there[:, :, None, None], far_terms[f - 1], merged)
        parts += [merged[0]] + [along_z(merged[s], -s) for s in range(1, places)]
    posterior, logs = weigh(me, parts, places, CHUNKS)
    return posterior, logs.reshape(-1)


def solution(mesh):
    placed = (
        P(("groups", "cls", "proj"), None),
        P(("groups", "cls", "proj"), None),
        P(("groups", "cls", "proj"), None),
        P(("groups", "cls", "proj"), None),
        P(("groups", "cls", "proj")),
        P("cls", "proj", None),
    )
    return jax.shard_map(
        per_device,
        mesh=mesh,
        in_specs=placed,
        out_specs=(P(("groups", "cls", "proj"), None, None), P(("groups", "cls", "proj"))),
        check_vma=False,
    )
```

```python
import functools
import math

import jax
import jax.numpy as jnp
from jax import lax
from jax.experimental import pallas as pl
from jax.experimental.pallas import tpu as pltpu
from jax.sharding import PartitionSpec as P

IMG = 64
KF = 2048
J = 2048
NB = 16
SW = 4
SH = 16
LANES = 128
WIDTH = 2 * KF + LANES
HALVES = 2 * KF // LANES
TILE = 8
TURN = 1024
GROUP = 4
BLOCK = J // NB
CHUNKS = 2
BF16_MAX = float(jnp.finfo(jnp.bfloat16).max)


def unit_circle(turn):
    turn = turn - IMG * jnp.floor(turn * (1.0 / IMG) + 0.5)
    half = turn * (math.pi / IMG)
    square = half * half
    sine, cosine = jnp.zeros_like(half), jnp.zeros_like(half)
    for n in (13, 11, 9, 7, 5, 3, 1):
        sine = sine * square + (-1.0) ** (n // 2) / math.factorial(n)
    for n in (14, 12, 10, 8, 6, 4, 2, 0):
        cosine = cosine * square + (-1.0) ** (n // 2) / math.factorial(n)
    sine = sine * half
    return 1.0 - 2.0 * sine * sine, 2.0 * sine * cosine


def pack_kernel(particles_ref, classes_ref, windows_ref, poses_ref, noise_ref, *refs):
    outs, facts = refs[:-1], refs[-1]
    count = particles_ref.shape[0]
    held = NB + 4 + 4
    line = lax.broadcasted_iota(jnp.int32, (held, count), 0)

    def spread(row):
        return jnp.broadcast_to(row, (held, count))

    column = jnp.where(line == 0, spread(classes_ref[...]).astype(jnp.float32), 0.0)
    column = jnp.where(line == 1, spread(windows_ref[0:1, :]).astype(jnp.float32), column)
    column = jnp.where(line == 2, spread(windows_ref[1:2, :]).astype(jnp.float32), column)
    column = jnp.where(line == 3, spread(noise_ref[...].astype(jnp.float32)), column)
    for n in range(poses_ref.shape[0]):
        column = jnp.where(line == spread(poses_ref[n:n + 1, :]) + 4, 1.0, column)
    facts[...] = jnp.zeros(facts.shape, jnp.float32)
    facts[0:held, 0:count] = column
    tail = facts[...].T[0:count, :].astype(jnp.bfloat16)
    part = count // len(outs)
    for j, out_ref in enumerate(outs):
        out_ref[:, 0:2 * KF] = particles_ref[j * part:(j + 1) * part, :]
        out_ref[:, 2 * KF:] = tail[j * part:(j + 1) * part, :]


def pack(particles, classes, windows, pose_lists, inverse_noise):
    count = particles.shape[0]
    whole = pl.BlockSpec(memory_space=pltpu.VMEM)
    return pl.pallas_call(
        pack_kernel,
        out_shape=[jax.ShapeDtypeStruct((count // CHUNKS, WIDTH), jnp.bfloat16)] * CHUNKS,
        in_specs=[whole] * 5,
        out_specs=[whole] * CHUNKS,
        scratch_shapes=[pltpu.VMEM((LANES, LANES), jnp.float32)],
        name="pack",
    )(particles, classes.T, windows.T, pose_lists.T, inverse_noise[None, :])


def turn_kernel(own_ref, other_ref, own_out, other_out, cos_ref, sin_ref):
    own_out[...] = own_ref[...].T
    other_out[...] = other_ref[...].T

    @pl.when(pl.program_id(0) == 0)
    def _():
        shift = lax.broadcasted_iota(jnp.int32, cos_ref.shape, 0)
        c = lax.broadcasted_iota(jnp.int32, cos_ref.shape, 1)
        kx, ky = c % IMG - IMG // 2, c // IMG
        turn = (shift % SW - SW // 2) * kx + (shift // SW - SW // 2) * ky
        cos_ref[...], sin_ref[...] = unit_circle(turn.astype(jnp.float32))


def turn(own_panel, other_panel):
    depth, width = own_panel.shape
    turned = jax.ShapeDtypeStruct((width, depth), own_panel.dtype)
    table = jax.ShapeDtypeStruct((SH, KF), jnp.float32)
    fixed = pl.BlockSpec((SH, KF), lambda i: (0, 0))
    return pl.pallas_call(
        turn_kernel,
        grid=(width // TURN,),
        out_shape=[turned, turned, table, table],
        in_specs=[pl.BlockSpec((depth, TURN), lambda i: (0, i))] * 2,
        out_specs=[pl.BlockSpec((TURN, depth), lambda i: (i, 0))] * 2 + [fixed] * 2,
        compiler_params=pltpu.CompilerParams(vmem_limit_bytes=20 * 1024 * 1024),
        cost_estimate=pl.CostEstimate(flops=0, bytes_accessed=16 << 20, transcendentals=0),
        name="turn",
    )(own_panel, other_panel)


def score_kernel(
    me_ref, rows_ref, own_any, other_any, cos_ref, sin_ref, out_ref,
    centred, shifted, scores, details, facts, members, panels, fact_sem, panel_sems,
):
    pieces, count, _ = rows_ref.shape
    for s in range(pieces):
        details[s * count:(s + 1) * count, :] = rows_ref[s, :, 2 * KF:].astype(jnp.float32)
    send = pltpu.make_async_copy(details, facts, fact_sem)
    send.start()
    loads = [
        pltpu.make_async_copy(panel, panels.at[n], panel_sems.at[n])
        for n, panel in enumerate((own_any, other_any))
    ]
    for copy in loads:
        copy.start()

    lane = lax.broadcasted_iota(jnp.int32, (count, LANES), 1)
    kx = (lane % IMG - IMG // 2).astype(jnp.float32)
    odd = (lane // IMG).astype(jnp.float32)
    for s in range(pieces):
        fact = details[s * count:(s + 1) * count, :]
        wx = jnp.broadcast_to(fact[:, 1:2], (count, LANES))
        wy = jnp.broadcast_to(fact[:, 2:3], (count, LANES))
        cosine, sine = unit_circle(wx * kx + wy * odd)
        step_cos, step_sin = unit_circle(wy * 2.0)
        for t in range(KF // LANES):
            at = slice(t * LANES, (t + 1) * LANES)
            to = slice(KF + t * LANES, KF + (t + 1) * LANES)
            re = rows_ref[s, :, at].astype(jnp.float32)
            im = rows_ref[s, :, to].astype(jnp.float32)
            centred[pl.ds(s * count * HALVES + t, count, HALVES), :] = re * cosine + im * sine
            centred[pl.ds(s * count * HALVES + HALVES // 2 + t, count, HALVES), :] = im * cosine - re * sine
            cosine, sine = (
                cosine * step_cos - sine * step_sin,
                sine * step_cos + cosine * step_sin,
            )
    send.wait()

    own = me_ref[0].astype(jnp.float32)
    other = (me_ref[0] ^ 1).astype(jnp.float32)
    first_block = me_ref[1]

    def sort_row(row, filled):
        label = facts[row, 0]
        members[0, filled[0]] = row
        members[1, filled[1]] = row
        return (
            filled[0] + (label == own).astype(jnp.int32),
            filled[1] + (label == other).astype(jnp.int32),
        )

    totals = lax.fori_loop(0, pieces * count, sort_row, (jnp.int32(0), jnp.int32(0)))

    for which, copy in enumerate(loads):
        copy.wait()

        @pl.loop(0, (totals[which] + TILE - 1) // TILE)
        def _(tile):
            base = tile * TILE
            present = jnp.minimum(totals[which] - base, TILE)

            spots = []
            for q in range(TILE):
                row = jnp.where(q < present, members[which, base + q], 0)
                spots.append(pl.multiple_of(row * HALVES, HALVES))
            for t in range(KF // LANES):
                at = slice(t * LANES, (t + 1) * LANES)
                to = slice(KF + t * LANES, KF + (t + 1) * LANES)
                cosine, sine = cos_ref[:, at], sin_ref[:, at]
                for q in range(TILE):
                    place = slice(q * SH, (q + 1) * SH)
                    base_re = spots[q] + t // 8 * 8
                    re = centred[pl.ds(pl.multiple_of(base_re, 8), 8), :][t % 8:t % 8 + 1, :]
                    im = centred[pl.ds(pl.multiple_of(base_re + HALVES // 2, 8), 8), :][t % 8:t % 8 + 1, :]
                    re = jnp.broadcast_to(re, (SH, LANES))
                    im = jnp.broadcast_to(im, (SH, LANES))
                    shifted[place, at] = (re * cosine + im * sine).astype(jnp.bfloat16)
                    shifted[place, to] = (im * cosine - re * sine).astype(jnp.bfloat16)

            scores[...] = jnp.dot(shifted[...], panels[which], preferred_element_type=jnp.float32)

            @pl.loop(0, present)
            def _(q):
                row = members[which, base + q]
                noise = facts[row, 3]
                place = pl.ds(pl.multiple_of(q * SH, SH), SH)
                for b in range(out_ref.shape[3] // BLOCK):
                    at = slice(b * BLOCK, (b + 1) * BLOCK)
                    allowed = facts[row, 4 + first_block + b]
                    term = jnp.minimum(jnp.exp(scores[place, at] * noise), BF16_MAX)
                    out_ref[row // count, row % count, :, at] = (term * allowed).astype(jnp.bfloat16)


def score(me, rows, own_panel, other_panel, cosine, sine):
    pieces, count, _ = rows.shape
    depth = own_panel.shape[1]
    total = pieces * count
    return pl.pallas_call(
        score_kernel,
        out_shape=jax.ShapeDtypeStruct((pieces, count, SH, depth), jnp.bfloat16),
        in_specs=[
            pl.BlockSpec(memory_space=pltpu.SMEM),
            pl.BlockSpec(memory_space=pltpu.VMEM),
            pl.BlockSpec(memory_space=pl.ANY),
            pl.BlockSpec(memory_space=pl.ANY),
            pl.BlockSpec(memory_space=pltpu.VMEM),
            pl.BlockSpec(memory_space=pltpu.VMEM),
        ],
        out_specs=pl.BlockSpec(memory_space=pltpu.VMEM),
        scratch_shapes=[
            pltpu.VMEM((total * HALVES, LANES), jnp.float32),
            pltpu.VMEM((TILE * SH, 2 * KF), jnp.bfloat16),
            pltpu.VMEM((TILE * SH, depth), jnp.float32),
            pltpu.VMEM((total, LANES), jnp.float32),
            pltpu.SMEM((total, LANES), jnp.float32),
            pltpu.SMEM((2, total + TILE), jnp.int32),
            pltpu.VMEM((2, 2 * KF, depth), jnp.bfloat16),
            pltpu.SemaphoreType.DMA,
            pltpu.SemaphoreType.DMA((2,)),
        ],
        compiler_params=pltpu.CompilerParams(vmem_limit_bytes=24 * 1024 * 1024),
        cost_estimate=pl.CostEstimate(
            flops=total * SH * depth * 4 * KF, bytes_accessed=16 << 20, transcendentals=0
        ),
        name="score",
    )(me, rows, own_panel, other_panel, cosine, sine)


def weigh_kernel(places, first, me_ref, *refs):
    parts, (weights_ref, log_ref) = refs[:places], refs[-2:]
    group, _, depth = parts[0].shape
    step = pl.program_id(0)

    @pl.when(step == 0)
    def _():
        log_ref[...] = refs[places + 1][...] if first else jnp.zeros(log_ref.shape, jnp.float32)

    lane = lax.broadcasted_iota(jnp.int32, log_ref.shape, 1)
    logs = log_ref[...]
    for g in range(group):
        total = sum(part[g].astype(jnp.float32) for part in parts)
        mean = jnp.sum(total, keepdims=True) / (SH * J)
        scale = 1.0 / mean
        for s in range(places):
            at = pl.multiple_of((me_ref[2] ^ s) * depth, depth)
            weights_ref[g, :, pl.ds(at, depth)] = parts[s][g].astype(jnp.float32) * scale
        logs = jnp.where(lane == first + step * group + g, jnp.log(mean), logs)
    log_ref[...] = logs


def weigh(me, parts, first, rows, before):
    places = len(parts)
    count, _, depth = parts[0].shape
    group = min(GROUP, count)
    logs = pl.BlockSpec((1, rows), lambda i: (0, 0))
    return pl.pallas_call(
        functools.partial(weigh_kernel, places, first),
        grid=(count // group,),
        out_shape=(
            jax.ShapeDtypeStruct((rows, SH, J), jnp.float32),
            jax.ShapeDtypeStruct((1, rows), jnp.float32),
        ),
        in_specs=[pl.BlockSpec(memory_space=pltpu.SMEM)]
        + [pl.BlockSpec((group, SH, depth), lambda i: (i, 0, 0))] * places
        + [pl.BlockSpec(memory_space=pl.ANY), logs][:len(before)],
        out_specs=(pl.BlockSpec((group, SH, J), lambda i: (first // group + i, 0, 0)), logs),
        input_output_aliases={places + 1: 0} if before else {},
        compiler_params=pltpu.CompilerParams(vmem_limit_bytes=16 * 1024 * 1024),
        name="weigh",
    )(me, *parts, *before)


def per_device(particles, classes, windows, pose_lists, inverse_noise, projections):
    owners = lax.axis_size("cls")
    places = lax.axis_size("proj")
    pairs = owners // 2
    label, place = lax.axis_index("cls"), lax.axis_index("proj")
    own_x = label // 2
    depth = projections.shape[1]
    me = jnp.stack([label, place * (depth // BLOCK), place]).astype(jnp.int32)

    def along_x(value, by):
        return lax.ppermute(value, "cls", [(i, i ^ (2 * by)) for i in range(owners)])

    def along_z(value, by):
        return lax.ppermute(value, "proj", [(i, i ^ by) for i in range(places)])

    chunks = pack(particles, classes, windows, pose_lists, inverse_noise)
    pieces = [[mine] + [along_z(mine, s) for s in range(1, places)] for mine in chunks]
    other_panel = lax.ppermute(projections[0], "cls", [(i, i ^ 1) for i in range(owners)])
    panels = turn(projections[0], other_panel)
    panels, pieces[1] = lax.optimization_barrier((panels, pieces[1]))
    columns = [jnp.stack(piece) for piece in pieces]
    far = [[along_x(column, f) for f in range(1, pairs)] for column in columns]
    near_terms = [score(me, columns[0], *panels)]
    far[0], near_terms[0], columns[1:] = lax.optimization_barrier((far[0], near_terms[0], columns[1:]))
    far_terms = []
    for group in far:
        terms = [score(me, rows, *panels) for rows in group]
        far_terms.append([along_x(t, f + 1) for f, t in enumerate(terms)])
    for column in columns[1:]:
        column, _ = lax.optimization_barrier((column, terms))
        near_terms.append(score(me, column, *panels))
    done = ()
    for j, column in enumerate(columns):
        if j:
            far_terms[j], parts = lax.optimization_barrier((far_terms[j], parts))
            done = weigh(me, parts, (j - 1) * column.shape[1], particles.shape[0], done)
        merged = near_terms[j]
        owner_x = column[:, :, 2 * KF].astype(jnp.int32) // 2
        for f in range(1, pairs):
            there = owner_x == (own_x ^ f)
            merged = jnp.where(there[:, :, None, None], far_terms[j][f - 1], merged)
        parts = [merged[0]] + [along_z(merged[s], s) for s in range(1, places)]
    done = weigh(me, parts, (CHUNKS - 1) * column.shape[1], particles.shape[0], done)
    return done[0], done[1].reshape(-1)


def solution(mesh):
    placed = (
        P(("groups", "cls", "proj"), None),
        P(("groups", "cls", "proj"), None),
        P(("groups", "cls", "proj"), None),
        P(("groups", "cls", "proj"), None),
        P(("groups", "cls", "proj")),
        P("cls", "proj", None),
    )
    return jax.shard_map(
        per_device,
        mesh=mesh,
        in_specs=placed,
        out_specs=(P(("groups", "cls", "proj"), None, None), P(("groups", "cls", "proj"))),
        check_vma=False,
    )
```

```python
import functools
import math

import jax
import jax.numpy as jnp
from jax import lax
from jax.experimental import pallas as pl
from jax.experimental.pallas import tpu as pltpu
from jax.sharding import PartitionSpec as P

IMG = 64
KF = 2048
J = 2048
NB = 16
SW = 4
SH = 16
LANES = 128
WIDTH = 2 * KF + LANES
HALVES = 2 * KF // LANES
TILE = 8
TURN = 1024
GROUP = 4
BLOCK = J // NB
CHUNKS = 2
BF16_MAX = float(jnp.finfo(jnp.bfloat16).max)


def unit_circle(turn):
    turn = turn - IMG * jnp.floor(turn * (1.0 / IMG) + 0.5)
    half = turn * (math.pi / IMG)
    square = half * half
    sine, cosine = jnp.zeros_like(half), jnp.zeros_like(half)
    for n in (13, 11, 9, 7, 5, 3, 1):
        sine = sine * square + (-1.0) ** (n // 2) / math.factorial(n)
    for n in (14, 12, 10, 8, 6, 4, 2, 0):
        cosine = cosine * square + (-1.0) ** (n // 2) / math.factorial(n)
    sine = sine * half
    return 1.0 - 2.0 * sine * sine, 2.0 * sine * cosine


def pack_kernel(particles_ref, classes_ref, windows_ref, poses_ref, noise_ref, *refs):
    outs, facts = refs[:-1], refs[-1]
    count = particles_ref.shape[0]
    held = NB + 4 + 4
    line = lax.broadcasted_iota(jnp.int32, (held, count), 0)

    def spread(row):
        return jnp.broadcast_to(row, (held, count))

    column = jnp.where(line == 0, spread(classes_ref[...]).astype(jnp.float32), 0.0)
    column = jnp.where(line == 1, spread(windows_ref[0:1, :]).astype(jnp.float32), column)
    column = jnp.where(line == 2, spread(windows_ref[1:2, :]).astype(jnp.float32), column)
    column = jnp.where(line == 3, spread(noise_ref[...].astype(jnp.float32)), column)
    for n in range(poses_ref.shape[0]):
        column = jnp.where(line == spread(poses_ref[n:n + 1, :]) + 4, 1.0, column)
    facts[...] = jnp.zeros(facts.shape, jnp.float32)
    facts[0:held, 0:count] = column
    tail = facts[...].T[0:count, :].astype(jnp.bfloat16)
    part = count // len(outs)
    for j, out_ref in enumerate(outs):
        out_ref[:, 0:2 * KF] = particles_ref[j * part:(j + 1) * part, :]
        out_ref[:, 2 * KF:] = tail[j * part:(j + 1) * part, :]


def pack(particles, classes, windows, pose_lists, inverse_noise):
    count = particles.shape[0]
    whole = pl.BlockSpec(memory_space=pltpu.VMEM)
    return pl.pallas_call(
        pack_kernel,
        out_shape=[jax.ShapeDtypeStruct((count // CHUNKS, WIDTH), jnp.bfloat16)] * CHUNKS,
        in_specs=[whole] * 5,
        out_specs=[whole] * CHUNKS,
        scratch_shapes=[pltpu.VMEM((LANES, LANES), jnp.float32)],
        name="pack",
    )(particles, classes.T, windows.T, pose_lists.T, inverse_noise[None, :])


def turn_kernel(own_ref, other_ref, own_out, other_out, cos_ref, sin_ref):
    own_out[...] = own_ref[...].T
    other_out[...] = other_ref[...].T

    @pl.when(pl.program_id(0) == 0)
    def _():
        shift = lax.broadcasted_iota(jnp.int32, cos_ref.shape, 0)
        c = lax.broadcasted_iota(jnp.int32, cos_ref.shape, 1)
        kx, ky = c % IMG - IMG // 2, c // IMG
        turn = (shift % SW - SW // 2) * kx + (shift // SW - SW // 2) * ky
        cos_ref[...], sin_ref[...] = unit_circle(turn.astype(jnp.float32))


def turn(own_panel, other_panel):
    depth, width = own_panel.shape
    turned = jax.ShapeDtypeStruct((width, depth), own_panel.dtype)
    table = jax.ShapeDtypeStruct((SH, KF), jnp.float32)
    fixed = pl.BlockSpec((SH, KF), lambda i: (0, 0))
    return pl.pallas_call(
        turn_kernel,
        grid=(width // TURN,),
        out_shape=[turned, turned, table, table],
        in_specs=[pl.BlockSpec((depth, TURN), lambda i: (0, i))] * 2,
        out_specs=[pl.BlockSpec((TURN, depth), lambda i: (i, 0))] * 2 + [fixed] * 2,
        compiler_params=pltpu.CompilerParams(vmem_limit_bytes=20 * 1024 * 1024),
        cost_estimate=pl.CostEstimate(flops=0, bytes_accessed=16 << 20, transcendentals=0),
        name="turn",
    )(own_panel, other_panel)


def score_kernel(
    me_ref, rows_ref, own_any, other_any, cos_ref, sin_ref, out_ref,
    centred, shifted, scores, details, facts, members, panels, fact_sem, panel_sems,
):
    pieces, count, _ = rows_ref.shape
    for s in range(pieces):
        details[s * count:(s + 1) * count, :] = rows_ref[s, :, 2 * KF:].astype(jnp.float32)
    send = pltpu.make_async_copy(details, facts, fact_sem)
    send.start()
    loads = [
        pltpu.make_async_copy(panel, panels.at[n], panel_sems.at[n])
        for n, panel in enumerate((own_any, other_any))
    ]
    for copy in loads:
        copy.start()

    lane = lax.broadcasted_iota(jnp.int32, (count, LANES), 1)
    kx = (lane % IMG - IMG // 2).astype(jnp.float32)
    odd = (lane // IMG).astype(jnp.float32)
    for s in range(pieces):
        fact = details[s * count:(s + 1) * count, :]
        wx = jnp.broadcast_to(fact[:, 1:2], (count, LANES))
        wy = jnp.broadcast_to(fact[:, 2:3], (count, LANES))
        cosine, sine = unit_circle(wx * kx + wy * odd)
        step_cos, step_sin = unit_circle(wy * 2.0)
        for t in range(KF // LANES):
            at = slice(t * LANES, (t + 1) * LANES)
            to = slice(KF + t * LANES, KF + (t + 1) * LANES)
            re = rows_ref[s, :, at].astype(jnp.float32)
            im = rows_ref[s, :, to].astype(jnp.float32)
            centred[pl.ds(s * count * HALVES + t, count, HALVES), :] = re * cosine + im * sine
            centred[pl.ds(s * count * HALVES + HALVES // 2 + t, count, HALVES), :] = im * cosine - re * sine
            cosine, sine = (
                cosine * step_cos - sine * step_sin,
                sine * step_cos + cosine * step_sin,
            )
    send.wait()

    own = me_ref[0].astype(jnp.float32)
    other = (me_ref[0] ^ 1).astype(jnp.float32)
    first_block = me_ref[1]

    def sort_row(row, filled):
        label = facts[row, 0]
        members[0, filled[0]] = row
        members[1, filled[1]] = row
        return (
            filled[0] + (label == own).astype(jnp.int32),
            filled[1] + (label == other).astype(jnp.int32),
        )

    totals = lax.fori_loop(0, pieces * count, sort_row, (jnp.int32(0), jnp.int32(0)), unroll=8)

    for which, copy in enumerate(loads):
        copy.wait()

        @pl.loop(0, (totals[which] + TILE - 1) // TILE)
        def _(tile):
            base = tile * TILE
            present = jnp.minimum(totals[which] - base, TILE)

            spots = []
            for q in range(TILE):
                row = jnp.where(q < present, members[which, base + q], 0)
                spots.append(pl.multiple_of(row * HALVES, HALVES))
            for t in range(KF // LANES):
                at = slice(t * LANES, (t + 1) * LANES)
                to = slice(KF + t * LANES, KF + (t + 1) * LANES)
                cosine, sine = cos_ref[:, at], sin_ref[:, at]
                for q in range(TILE):
                    place = slice(q * SH, (q + 1) * SH)
                    base_re = spots[q] + t // 8 * 8
                    re = centred[pl.ds(pl.multiple_of(base_re, 8), 8), :][t % 8:t % 8 + 1, :]
                    im = centred[pl.ds(pl.multiple_of(base_re + HALVES // 2, 8), 8), :][t % 8:t % 8 + 1, :]
                    re = jnp.broadcast_to(re, (SH, LANES))
                    im = jnp.broadcast_to(im, (SH, LANES))
                    shifted[place, at] = (re * cosine + im * sine).astype(jnp.bfloat16)
                    shifted[place, to] = (im * cosine - re * sine).astype(jnp.bfloat16)

            scores[...] = jnp.dot(shifted[...], panels[which], preferred_element_type=jnp.float32)

            @pl.loop(0, present)
            def _(q):
                row = members[which, base + q]
                noise = facts[row, 3]
                place = pl.ds(pl.multiple_of(q * SH, SH), SH)
                for b in range(out_ref.shape[3] // BLOCK):
                    at = slice(b * BLOCK, (b + 1) * BLOCK)
                    allowed = facts[row, 4 + first_block + b]
                    term = jnp.minimum(jnp.exp(scores[place, at] * noise), BF16_MAX)
                    out_ref[row // count, row % count, :, at] = (term * allowed).astype(jnp.bfloat16)


def score(me, rows, own_panel, other_panel, cosine, sine):
    pieces, count, _ = rows.shape
    depth = own_panel.shape[1]
    total = pieces * count
    return pl.pallas_call(
        score_kernel,
        out_shape=jax.ShapeDtypeStruct((pieces, count, SH, depth), jnp.bfloat16),
        in_specs=[
            pl.BlockSpec(memory_space=pltpu.SMEM),
            pl.BlockSpec(memory_space=pltpu.VMEM),
            pl.BlockSpec(memory_space=pl.ANY),
            pl.BlockSpec(memory_space=pl.ANY),
            pl.BlockSpec(memory_space=pltpu.VMEM),
            pl.BlockSpec(memory_space=pltpu.VMEM),
        ],
        out_specs=pl.BlockSpec(memory_space=pltpu.VMEM),
        scratch_shapes=[
            pltpu.VMEM((total * HALVES, LANES), jnp.float32),
            pltpu.VMEM((TILE * SH, 2 * KF), jnp.bfloat16),
            pltpu.VMEM((TILE * SH, depth), jnp.float32),
            pltpu.VMEM((total, LANES), jnp.float32),
            pltpu.SMEM((total, LANES), jnp.float32),
            pltpu.SMEM((2, total + TILE), jnp.int32),
            pltpu.VMEM((2, 2 * KF, depth), jnp.bfloat16),
            pltpu.SemaphoreType.DMA,
            pltpu.SemaphoreType.DMA((2,)),
        ],
        compiler_params=pltpu.CompilerParams(vmem_limit_bytes=24 * 1024 * 1024),
        cost_estimate=pl.CostEstimate(
            flops=total * SH * depth * 4 * KF, bytes_accessed=16 << 20, transcendentals=0
        ),
        name="score",
    )(me, rows, own_panel, other_panel, cosine, sine)


def weigh_kernel(places, first, me_ref, *refs):
    parts, (weights_ref, log_ref) = refs[:places], refs[-2:]
    group, _, depth = parts[0].shape
    step = pl.program_id(0)

    @pl.when(step == 0)
    def _():
        log_ref[...] = refs[places + 1][...] if first else jnp.zeros(log_ref.shape, jnp.float32)

    lane = lax.broadcasted_iota(jnp.int32, log_ref.shape, 1)
    logs = log_ref[...]
    for g in range(group):
        total = sum(part[g].astype(jnp.float32) for part in parts)
        mean = jnp.sum(total, keepdims=True) / (SH * J)
        scale = 1.0 / mean
        for s in range(places):
            at = pl.multiple_of((me_ref[2] ^ s) * depth, depth)
            weights_ref[g, :, pl.ds(at, depth)] = parts[s][g].astype(jnp.float32) * scale
        logs = jnp.where(lane == first + step * group + g, jnp.log(mean), logs)
    log_ref[...] = logs


def weigh(me, parts, first, rows, before):
    places = len(parts)
    count, _, depth = parts[0].shape
    group = min(GROUP, count)
    logs = pl.BlockSpec((1, rows), lambda i: (0, 0))
    return pl.pallas_call(
        functools.partial(weigh_kernel, places, first),
        grid=(count // group,),
        out_shape=(
            jax.ShapeDtypeStruct((rows, SH, J), jnp.float32),
            jax.ShapeDtypeStruct((1, rows), jnp.float32),
        ),
        in_specs=[pl.BlockSpec(memory_space=pltpu.SMEM)]
        + [pl.BlockSpec((group, SH, depth), lambda i: (i, 0, 0))] * places
        + [pl.BlockSpec(memory_space=pl.ANY), logs][:len(before)],
        out_specs=(pl.BlockSpec((group, SH, J), lambda i: (first // group + i, 0, 0)), logs),
        input_output_aliases={places + 1: 0} if before else {},
        compiler_params=pltpu.CompilerParams(vmem_limit_bytes=16 * 1024 * 1024),
        name="weigh",
    )(me, *parts, *before)


def per_device(particles, classes, windows, pose_lists, inverse_noise, projections):
    owners = lax.axis_size("cls")
    places = lax.axis_size("proj")
    pairs = owners // 2
    label, place = lax.axis_index("cls"), lax.axis_index("proj")
    own_x = label // 2
    depth = projections.shape[1]
    me = jnp.stack([label, place * (depth // BLOCK), place]).astype(jnp.int32)

    def along_x(value, by):
        return lax.ppermute(value, "cls", [(i, i ^ (2 * by)) for i in range(owners)])

    def along_z(value, by):
        return lax.ppermute(value, "proj", [(i, i ^ by) for i in range(places)])

    chunks = pack(particles, classes, windows, pose_lists, inverse_noise)
    pieces = [[mine] + [along_z(mine, s) for s in range(1, places)] for mine in chunks]
    other_panel = lax.ppermute(projections[0], "cls", [(i, i ^ 1) for i in range(owners)])
    panels = turn(projections[0], other_panel)
    panels, pieces[1] = lax.optimization_barrier((panels, pieces[1]))
    columns = [jnp.stack(piece) for piece in pieces]
    far = [[along_x(column, f) for f in range(1, pairs)] for column in columns]
    far[0], columns[1:] = lax.optimization_barrier((far[0], columns[1:]))
    far_terms = []
    for group in far:
        terms = [score(me, rows, *panels) for rows in group]
        far_terms.append([along_x(t, f + 1) for f, t in enumerate(terms)])
    done, parts = (), None
    for j, column in enumerate(columns):
        column, terms = lax.optimization_barrier((column, terms))
        merged = score(me, column, *panels)
        owner_x = column[:, :, 2 * KF].astype(jnp.int32) // 2
        if j:
            far_terms[j], parts = lax.optimization_barrier((far_terms[j], parts))
            done = weigh(me, parts, (j - 1) * column.shape[1], particles.shape[0], done)
        for f in range(1, pairs):
            there = owner_x == (own_x ^ f)
            merged = jnp.where(there[:, :, None, None], far_terms[j][f - 1], merged)
        terms = merged
        parts = [merged[0]] + [along_z(merged[s], s) for s in range(1, places)]
    done = weigh(me, parts, (CHUNKS - 1) * column.shape[1], particles.shape[0], done)
    return done[0], done[1].reshape(-1)


def solution(mesh):
    placed = (
        P(("groups", "cls", "proj"), None),
        P(("groups", "cls", "proj"), None),
        P(("groups", "cls", "proj"), None),
        P(("groups", "cls", "proj"), None),
        P(("groups", "cls", "proj")),
        P("cls", "proj", None),
    )
    return jax.shard_map(
        per_device,
        mesh=mesh,
        in_specs=placed,
        out_specs=(P(("groups", "cls", "proj"), None, None), P(("groups", "cls", "proj"))),
        check_vma=False,
    )
```

```python
import functools
import math

import jax
import jax.numpy as jnp
from jax import lax
from jax.experimental import pallas as pl
from jax.experimental.pallas import tpu as pltpu
from jax.sharding import PartitionSpec as P

IMG = 64
KF = 2048
J = 2048
NB = 16
SW = 4
SH = 16
LANES = 128
WIDTH = 2 * KF + LANES
HALVES = 2 * KF // LANES
TILE = 8
TURN = 1024
GROUP = 4
BLOCK = J // NB
CHUNKS = 2
BF16_MAX = float(jnp.finfo(jnp.bfloat16).max)


def unit_circle(turn):
    turn = turn - IMG * jnp.floor(turn * (1.0 / IMG) + 0.5)
    half = turn * (math.pi / IMG)
    square = half * half
    sine, cosine = jnp.zeros_like(half), jnp.zeros_like(half)
    for n in (13, 11, 9, 7, 5, 3, 1):
        sine = sine * square + (-1.0) ** (n // 2) / math.factorial(n)
    for n in (14, 12, 10, 8, 6, 4, 2, 0):
        cosine = cosine * square + (-1.0) ** (n // 2) / math.factorial(n)
    sine = sine * half
    return 1.0 - 2.0 * sine * sine, 2.0 * sine * cosine


def pack_kernel(particles_ref, classes_ref, windows_ref, poses_ref, noise_ref, *refs):
    outs, facts = refs[:-1], refs[-1]
    count = particles_ref.shape[0]
    held = NB + 4 + 4
    line = lax.broadcasted_iota(jnp.int32, (held, count), 0)

    def spread(row):
        return jnp.broadcast_to(row, (held, count))

    column = jnp.where(line == 0, spread(classes_ref[...]).astype(jnp.float32), 0.0)
    column = jnp.where(line == 1, spread(windows_ref[0:1, :]).astype(jnp.float32), column)
    column = jnp.where(line == 2, spread(windows_ref[1:2, :]).astype(jnp.float32), column)
    column = jnp.where(line == 3, spread(noise_ref[...].astype(jnp.float32)), column)
    for n in range(poses_ref.shape[0]):
        column = jnp.where(line == spread(poses_ref[n:n + 1, :]) + 4, 1.0, column)
    facts[...] = jnp.zeros(facts.shape, jnp.float32)
    facts[0:held, 0:count] = column
    tail = facts[...].T[0:count, :].astype(jnp.bfloat16)
    part = count // len(outs)
    for j, out_ref in enumerate(outs):
        out_ref[:, 0:2 * KF] = particles_ref[j * part:(j + 1) * part, :]
        out_ref[:, 2 * KF:] = tail[j * part:(j + 1) * part, :]


def pack(particles, classes, windows, pose_lists, inverse_noise):
    count = particles.shape[0]
    whole = pl.BlockSpec(memory_space=pltpu.VMEM)
    return pl.pallas_call(
        pack_kernel,
        out_shape=[jax.ShapeDtypeStruct((count // CHUNKS, WIDTH), jnp.bfloat16)] * CHUNKS,
        in_specs=[whole] * 5,
        out_specs=[whole] * CHUNKS,
        scratch_shapes=[pltpu.VMEM((LANES, LANES), jnp.float32)],
        name="pack",
    )(particles, classes.T, windows.T, pose_lists.T, inverse_noise[None, :])


def turn_kernel(own_ref, other_ref, own_out, other_out, cos_ref, sin_ref):
    own_out[...] = own_ref[...].T
    other_out[...] = other_ref[...].T

    @pl.when(pl.program_id(0) == 0)
    def _():
        shift = lax.broadcasted_iota(jnp.int32, cos_ref.shape, 0)
        c = lax.broadcasted_iota(jnp.int32, cos_ref.shape, 1)
        kx, ky = c % IMG - IMG // 2, c // IMG
        turn = (shift % SW - SW // 2) * kx + (shift // SW - SW // 2) * ky
        cos_ref[...], sin_ref[...] = unit_circle(turn.astype(jnp.float32))


def turn(own_panel, other_panel):
    depth, width = own_panel.shape
    turned = jax.ShapeDtypeStruct((width, depth), own_panel.dtype)
    table = jax.ShapeDtypeStruct((SH, KF), jnp.float32)
    fixed = pl.BlockSpec((SH, KF), lambda i: (0, 0))
    return pl.pallas_call(
        turn_kernel,
        grid=(width // TURN,),
        out_shape=[turned, turned, table, table],
        in_specs=[pl.BlockSpec((depth, TURN), lambda i: (0, i))] * 2,
        out_specs=[pl.BlockSpec((TURN, depth), lambda i: (i, 0))] * 2 + [fixed] * 2,
        compiler_params=pltpu.CompilerParams(vmem_limit_bytes=20 * 1024 * 1024),
        cost_estimate=pl.CostEstimate(flops=0, bytes_accessed=16 << 20, transcendentals=0),
        name="turn",
    )(own_panel, other_panel)


def score_kernel(
    me_ref, rows_ref, own_any, other_any, cos_ref, sin_ref, out_ref,
    centred, shifted, scores, details, facts, members, panels, fact_sem, panel_sems,
):
    pieces, count, _ = rows_ref.shape
    for s in range(pieces):
        details[s * count:(s + 1) * count, :] = rows_ref[s, :, 2 * KF:].astype(jnp.float32)
    send = pltpu.make_async_copy(details, facts, fact_sem)
    send.start()
    loads = [
        pltpu.make_async_copy(panel, panels.at[n], panel_sems.at[n])
        for n, panel in enumerate((own_any, other_any))
    ]
    for copy in loads:
        copy.start()

    lane = lax.broadcasted_iota(jnp.int32, (count, LANES), 1)
    kx = (lane % IMG - IMG // 2).astype(jnp.float32)
    odd = (lane // IMG).astype(jnp.float32)
    for s in range(pieces):
        fact = details[s * count:(s + 1) * count, :]
        wx = jnp.broadcast_to(fact[:, 1:2], (count, LANES))
        wy = jnp.broadcast_to(fact[:, 2:3], (count, LANES))
        cosine, sine = unit_circle(wx * kx + wy * odd)
        step_cos, step_sin = unit_circle(wy * 2.0)
        for t in range(KF // LANES):
            at = slice(t * LANES, (t + 1) * LANES)
            to = slice(KF + t * LANES, KF + (t + 1) * LANES)
            re = rows_ref[s, :, at].astype(jnp.float32)
            im = rows_ref[s, :, to].astype(jnp.float32)
            centred[pl.ds(s * count * HALVES + t, count, HALVES), :] = re * cosine + im * sine
            centred[pl.ds(s * count * HALVES + HALVES // 2 + t, count, HALVES), :] = im * cosine - re * sine
            cosine, sine = (
                cosine * step_cos - sine * step_sin,
                sine * step_cos + cosine * step_sin,
            )
    send.wait()

    own = me_ref[0].astype(jnp.float32)
    other = (me_ref[0] ^ 1).astype(jnp.float32)
    first_block = me_ref[1]

    def sort_row(row, filled):
        label = facts[row, 0]
        members[0, filled[0]] = row
        members[1, filled[1]] = row
        return (
            filled[0] + (label == own).astype(jnp.int32),
            filled[1] + (label == other).astype(jnp.int32),
        )

    totals = lax.fori_loop(0, pieces * count, sort_row, (jnp.int32(0), jnp.int32(0)), unroll=8)

    for which, copy in enumerate(loads):
        copy.wait()

        @pl.loop(0, (totals[which] + TILE - 1) // TILE)
        def _(tile):
            base = tile * TILE
            present = jnp.minimum(totals[which] - base, TILE)

            spots = []
            for q in range(TILE):
                row = jnp.where(q < present, members[which, base + q], 0)
                spots.append(pl.multiple_of(row * HALVES, HALVES))
            for t in range(KF // LANES):
                at = slice(t * LANES, (t + 1) * LANES)
                to = slice(KF + t * LANES, KF + (t + 1) * LANES)
                cosine, sine = cos_ref[:, at], sin_ref[:, at]
                for q in range(TILE):
                    place = slice(q * SH, (q + 1) * SH)
                    base_re = spots[q] + t // 8 * 8
                    re = centred[pl.ds(pl.multiple_of(base_re, 8), 8), :][t % 8:t % 8 + 1, :]
                    im = centred[pl.ds(pl.multiple_of(base_re + HALVES // 2, 8), 8), :][t % 8:t % 8 + 1, :]
                    re = jnp.broadcast_to(re, (SH, LANES))
                    im = jnp.broadcast_to(im, (SH, LANES))
                    shifted[place, at] = (re * cosine + im * sine).astype(jnp.bfloat16)
                    shifted[place, to] = (im * cosine - re * sine).astype(jnp.bfloat16)

            scores[...] = jnp.dot(shifted[...], panels[which], preferred_element_type=jnp.float32)

            @pl.loop(0, present)
            def _(q):
                row = members[which, base + q]
                noise = facts[row, 3]
                place = pl.ds(pl.multiple_of(q * SH, SH), SH)
                for b in range(out_ref.shape[3] // BLOCK):
                    at = slice(b * BLOCK, (b + 1) * BLOCK)
                    allowed = facts[row, 4 + first_block + b]
                    term = jnp.minimum(jnp.exp(scores[place, at] * noise), BF16_MAX)
                    out_ref[row // count, row % count, :, at] = (term * allowed).astype(jnp.bfloat16)


def score(me, rows, own_panel, other_panel, cosine, sine):
    pieces, count, _ = rows.shape
    depth = own_panel.shape[1]
    total = pieces * count
    return pl.pallas_call(
        score_kernel,
        out_shape=jax.ShapeDtypeStruct((pieces, count, SH, depth), jnp.bfloat16),
        in_specs=[
            pl.BlockSpec(memory_space=pltpu.SMEM),
            pl.BlockSpec(memory_space=pltpu.VMEM),
            pl.BlockSpec(memory_space=pl.ANY),
            pl.BlockSpec(memory_space=pl.ANY),
            pl.BlockSpec(memory_space=pltpu.VMEM),
            pl.BlockSpec(memory_space=pltpu.VMEM),
        ],
        out_specs=pl.BlockSpec(memory_space=pltpu.VMEM),
        scratch_shapes=[
            pltpu.VMEM((total * HALVES, LANES), jnp.float32),
            pltpu.VMEM((TILE * SH, 2 * KF), jnp.bfloat16),
            pltpu.VMEM((TILE * SH, depth), jnp.float32),
            pltpu.VMEM((total, LANES), jnp.float32),
            pltpu.SMEM((total, LANES), jnp.float32),
            pltpu.SMEM((2, total + TILE), jnp.int32),
            pltpu.VMEM((2, 2 * KF, depth), jnp.bfloat16),
            pltpu.SemaphoreType.DMA,
            pltpu.SemaphoreType.DMA((2,)),
        ],
        compiler_params=pltpu.CompilerParams(vmem_limit_bytes=24 * 1024 * 1024),
        cost_estimate=pl.CostEstimate(
            flops=total * SH * depth * 4 * KF, bytes_accessed=16 << 20, transcendentals=0
        ),
        name="score",
    )(me, rows, own_panel, other_panel, cosine, sine)


def weigh_kernel(places, first, me_ref, *refs):
    parts, (weights_ref, log_ref) = refs[:places], refs[-2:]
    group, _, depth = parts[0].shape
    step = pl.program_id(0)

    @pl.when(step == 0)
    def _():
        log_ref[...] = refs[places + 1][...] if first else jnp.zeros(log_ref.shape, jnp.float32)

    lane = lax.broadcasted_iota(jnp.int32, log_ref.shape, 1)
    logs = log_ref[...]
    for g in range(group):
        total = sum(part[g].astype(jnp.float32) for part in parts)
        mean = jnp.sum(total, keepdims=True) / (SH * J)
        scale = 1.0 / mean
        for s in range(places):
            at = pl.multiple_of((me_ref[2] ^ s) * depth, depth)
            weights_ref[g, :, pl.ds(at, depth)] = parts[s][g].astype(jnp.float32) * scale
        logs = jnp.where(lane == first + step * group + g, jnp.log(mean), logs)
    log_ref[...] = logs


def weigh(me, parts, first, rows, before):
    places = len(parts)
    count, _, depth = parts[0].shape
    group = min(GROUP, count)
    logs = pl.BlockSpec((1, rows), lambda i: (0, 0))
    return pl.pallas_call(
        functools.partial(weigh_kernel, places, first),
        grid=(count // group,),
        out_shape=(
            jax.ShapeDtypeStruct((rows, SH, J), jnp.float32),
            jax.ShapeDtypeStruct((1, rows), jnp.float32),
        ),
        in_specs=[pl.BlockSpec(memory_space=pltpu.SMEM)]
        + [pl.BlockSpec((group, SH, depth), lambda i: (i, 0, 0))] * places
        + [pl.BlockSpec(memory_space=pl.ANY), logs][:len(before)],
        out_specs=(pl.BlockSpec((group, SH, J), lambda i: (first // group + i, 0, 0)), logs),
        input_output_aliases={places + 1: 0} if before else {},
        compiler_params=pltpu.CompilerParams(vmem_limit_bytes=16 * 1024 * 1024),
        name="weigh",
    )(me, *parts, *before)


def per_device(particles, classes, windows, pose_lists, inverse_noise, projections):
    owners = lax.axis_size("cls")
    places = lax.axis_size("proj")
    pairs = owners // 2
    label, place = lax.axis_index("cls"), lax.axis_index("proj")
    own_x = label // 2
    depth = projections.shape[1]
    me = jnp.stack([label, place * (depth // BLOCK), place]).astype(jnp.int32)

    def along_x(value, by):
        return lax.ppermute(value, "cls", [(i, i ^ (2 * by)) for i in range(owners)])

    def along_z(value, by):
        return lax.ppermute(value, "proj", [(i, i ^ by) for i in range(places)])

    chunks = pack(particles, classes, windows, pose_lists, inverse_noise)
    pieces = [[mine] + [along_z(mine, s) for s in range(1, places)] for mine in chunks]
    other_panel = lax.ppermute(projections[0], "cls", [(i, i ^ 1) for i in range(owners)])
    panels = turn(projections[0], other_panel)
    panels, pieces[1] = lax.optimization_barrier((panels, pieces[1]))
    columns = [jnp.stack(piece) for piece in pieces]
    far = [[along_x(column, f) for f in range(1, pairs)] for column in columns]
    far[0], columns[1:] = lax.optimization_barrier((far[0], columns[1:]))
    far_terms = []
    for group in far:
        terms = [score(me, rows, *panels) for rows in group]
        far_terms.append([along_x(t, f + 1) for f, t in enumerate(terms)])
    done, parts = (), None
    for j, column in enumerate(columns):
        column, terms = lax.optimization_barrier((column, terms))
        merged = score(me, column, *panels)
        owner_x = column[:, :, 2 * KF].astype(jnp.int32) // 2
        if j:
            far_terms[j], parts[1] = lax.optimization_barrier((far_terms[j], parts[1]))
            done = weigh(me, parts, (j - 1) * column.shape[1], particles.shape[0], done)
        for f in range(1, pairs):
            there = owner_x == (own_x ^ f)
            merged = jnp.where(there[:, :, None, None], far_terms[j][f - 1], merged)
        terms = merged
        parts = [merged[0]] + [along_z(merged[s], s) for s in range(1, places)]
    done = weigh(me, parts, (CHUNKS - 1) * column.shape[1], particles.shape[0], done)
    return done[0], done[1].reshape(-1)


def solution(mesh):
    placed = (
        P(("groups", "cls", "proj"), None),
        P(("groups", "cls", "proj"), None),
        P(("groups", "cls", "proj"), None),
        P(("groups", "cls", "proj"), None),
        P(("groups", "cls", "proj")),
        P("cls", "proj", None),
    )
    return jax.shard_map(
        per_device,
        mesh=mesh,
        in_specs=placed,
        out_specs=(P(("groups", "cls", "proj"), None, None), P(("groups", "cls", "proj"))),
        check_vma=False,
    )
```

```python
import functools
import math

import jax
import jax.numpy as jnp
from jax import lax
from jax.experimental import pallas as pl
from jax.experimental.pallas import tpu as pltpu
from jax.sharding import PartitionSpec as P

IMG = 64
KF = 2048
J = 2048
NB = 16
SW = 4
SH = 16
LANES = 128
WIDTH = 2 * KF + LANES
HALVES = 2 * KF // LANES
TILE = 8
TURN = 1024
GROUP = 4
BLOCK = J // NB
CHUNKS = 2
BF16_MAX = float(jnp.finfo(jnp.bfloat16).max)


def unit_circle(turn):
    turn = turn - IMG * jnp.floor(turn * (1.0 / IMG) + 0.5)
    half = turn * (math.pi / IMG)
    square = half * half
    sine, cosine = jnp.zeros_like(half), jnp.zeros_like(half)
    for n in (13, 11, 9, 7, 5, 3, 1):
        sine = sine * square + (-1.0) ** (n // 2) / math.factorial(n)
    for n in (14, 12, 10, 8, 6, 4, 2, 0):
        cosine = cosine * square + (-1.0) ** (n // 2) / math.factorial(n)
    sine = sine * half
    return 1.0 - 2.0 * sine * sine, 2.0 * sine * cosine


def pack_kernel(particles_ref, classes_ref, windows_ref, poses_ref, noise_ref, *refs):
    outs, facts = refs[:-1], refs[-1]
    count = particles_ref.shape[0]
    held = NB + 4 + 4
    line = lax.broadcasted_iota(jnp.int32, (held, count), 0)

    def spread(row):
        return jnp.broadcast_to(row, (held, count))

    column = jnp.where(line == 0, spread(classes_ref[...]).astype(jnp.float32), 0.0)
    column = jnp.where(line == 1, spread(windows_ref[0:1, :]).astype(jnp.float32), column)
    column = jnp.where(line == 2, spread(windows_ref[1:2, :]).astype(jnp.float32), column)
    column = jnp.where(line == 3, spread(noise_ref[...].astype(jnp.float32)), column)
    for n in range(poses_ref.shape[0]):
        column = jnp.where(line == spread(poses_ref[n:n + 1, :]) + 4, 1.0, column)
    facts[...] = jnp.zeros(facts.shape, jnp.float32)
    facts[0:held, 0:count] = column
    tail = facts[...].T[0:count, :].astype(jnp.bfloat16)
    part = count // len(outs)
    for j, out_ref in enumerate(outs):
        out_ref[:, 0:2 * KF] = particles_ref[j * part:(j + 1) * part, :]
        out_ref[:, 2 * KF:] = tail[j * part:(j + 1) * part, :]


def pack(particles, classes, windows, pose_lists, inverse_noise):
    count = particles.shape[0]
    whole = pl.BlockSpec(memory_space=pltpu.VMEM)
    return pl.pallas_call(
        pack_kernel,
        out_shape=[jax.ShapeDtypeStruct((count // CHUNKS, WIDTH), jnp.bfloat16)] * CHUNKS,
        in_specs=[whole] * 5,
        out_specs=[whole] * CHUNKS,
        scratch_shapes=[pltpu.VMEM((LANES, LANES), jnp.float32)],
        name="pack",
    )(particles, classes.T, windows.T, pose_lists.T, inverse_noise[None, :])


def turn_kernel(own_any, other_any, own_out, other_out, cos_ref, sin_ref, blocks, sems):
    _, steps, _, width = blocks.shape
    loads = [
        pltpu.make_async_copy(panel.at[:, pl.ds(i * width, width)], blocks.at[n, i], sems.at[n, i])
        for n, panel in enumerate((own_any, other_any))
        for i in range(steps)
    ]
    for copy in loads:
        copy.start()
    shift = lax.broadcasted_iota(jnp.int32, cos_ref.shape, 0)
    c = lax.broadcasted_iota(jnp.int32, cos_ref.shape, 1)
    kx, ky = c % IMG - IMG // 2, c // IMG
    turn = (shift % SW - SW // 2) * kx + (shift // SW - SW // 2) * ky
    cos_ref[...], sin_ref[...] = unit_circle(turn.astype(jnp.float32))
    for n, out_ref in enumerate((own_out, other_out)):
        for i in range(steps):
            loads[n * steps + i].wait()
            out_ref[i * width:(i + 1) * width, :] = blocks[n, i].T


def turn(own_panel, other_panel):
    depth, width = own_panel.shape
    turned = jax.ShapeDtypeStruct((width, depth), own_panel.dtype)
    table = jax.ShapeDtypeStruct((SH, KF), jnp.float32)
    steps = width // TURN
    return pl.pallas_call(
        turn_kernel,
        out_shape=[turned, turned, table, table],
        in_specs=[pl.BlockSpec(memory_space=pl.ANY)] * 2,
        out_specs=[pl.BlockSpec(memory_space=pltpu.VMEM)] * 4,
        scratch_shapes=[
            pltpu.VMEM((2, steps, depth, TURN), jnp.bfloat16),
            pltpu.SemaphoreType.DMA((2, steps)),
        ],
        compiler_params=pltpu.CompilerParams(vmem_limit_bytes=20 * 1024 * 1024),
        cost_estimate=pl.CostEstimate(flops=1 << 32, bytes_accessed=0, transcendentals=0),
        name="turn",
    )(own_panel, other_panel)


def score_kernel(
    me_ref, rows_ref, own_any, other_any, cos_ref, sin_ref, out_ref,
    centred, shifted, scores, details, facts, members, panels, fact_sem, panel_sems,
):
    pieces, count, _ = rows_ref.shape
    for s in range(pieces):
        details[s * count:(s + 1) * count, :] = rows_ref[s, :, 2 * KF:].astype(jnp.float32)
    send = pltpu.make_async_copy(details, facts, fact_sem)
    send.start()
    loads = [
        pltpu.make_async_copy(panel, panels.at[n], panel_sems.at[n])
        for n, panel in enumerate((own_any, other_any))
    ]
    for copy in loads:
        copy.start()

    lane = lax.broadcasted_iota(jnp.int32, (count, LANES), 1)
    kx = (lane % IMG - IMG // 2).astype(jnp.float32)
    odd = (lane // IMG).astype(jnp.float32)
    for s in range(pieces):
        fact = details[s * count:(s + 1) * count, :]
        wx = jnp.broadcast_to(fact[:, 1:2], (count, LANES))
        wy = jnp.broadcast_to(fact[:, 2:3], (count, LANES))
        cosine, sine = unit_circle(wx * kx + wy * odd)
        step_cos, step_sin = unit_circle(wy * 2.0)
        for t in range(KF // LANES):
            at = slice(t * LANES, (t + 1) * LANES)
            to = slice(KF + t * LANES, KF + (t + 1) * LANES)
            re = rows_ref[s, :, at].astype(jnp.float32)
            im = rows_ref[s, :, to].astype(jnp.float32)
            centred[pl.ds(s * count * HALVES + t, count, HALVES), :] = re * cosine + im * sine
            centred[pl.ds(s * count * HALVES + HALVES // 2 + t, count, HALVES), :] = im * cosine - re * sine
            cosine, sine = (
                cosine * step_cos - sine * step_sin,
                sine * step_cos + cosine * step_sin,
            )
    send.wait()

    own = me_ref[0].astype(jnp.float32)
    other = (me_ref[0] ^ 1).astype(jnp.float32)
    first_block = me_ref[1]

    def sort_row(row, filled):
        label = facts[row, 0]
        members[0, filled[0]] = row
        members[1, filled[1]] = row
        return (
            filled[0] + (label == own).astype(jnp.int32),
            filled[1] + (label == other).astype(jnp.int32),
        )

    totals = lax.fori_loop(0, pieces * count, sort_row, (jnp.int32(0), jnp.int32(0)), unroll=8)

    for which, copy in enumerate(loads):
        copy.wait()

        @pl.loop(0, (totals[which] + TILE - 1) // TILE)
        def _(tile):
            base = tile * TILE
            present = jnp.minimum(totals[which] - base, TILE)

            spots = []
            for q in range(TILE):
                row = jnp.where(q < present, members[which, base + q], 0)
                spots.append(pl.multiple_of(row * HALVES, HALVES))
            for t in range(KF // LANES):
                at = slice(t * LANES, (t + 1) * LANES)
                to = slice(KF + t * LANES, KF + (t + 1) * LANES)
                cosine, sine = cos_ref[:, at], sin_ref[:, at]
                for q in range(TILE):
                    place = slice(q * SH, (q + 1) * SH)
                    base_re = spots[q] + t // 8 * 8
                    re = centred[pl.ds(pl.multiple_of(base_re, 8), 8), :][t % 8:t % 8 + 1, :]
                    im = centred[pl.ds(pl.multiple_of(base_re + HALVES // 2, 8), 8), :][t % 8:t % 8 + 1, :]
                    re = jnp.broadcast_to(re, (SH, LANES))
                    im = jnp.broadcast_to(im, (SH, LANES))
                    shifted[place, at] = (re * cosine + im * sine).astype(jnp.bfloat16)
                    shifted[place, to] = (im * cosine - re * sine).astype(jnp.bfloat16)

            scores[...] = jnp.dot(shifted[...], panels[which], preferred_element_type=jnp.float32)

            @pl.loop(0, present)
            def _(q):
                row = members[which, base + q]
                noise = facts[row, 3]
                place = pl.ds(pl.multiple_of(q * SH, SH), SH)
                for b in range(out_ref.shape[3] // BLOCK):
                    at = slice(b * BLOCK, (b + 1) * BLOCK)
                    allowed = facts[row, 4 + first_block + b]
                    term = jnp.minimum(jnp.exp(scores[place, at] * noise), BF16_MAX)
                    out_ref[row // count, row % count, :, at] = (term * allowed).astype(jnp.bfloat16)


def score(me, rows, own_panel, other_panel, cosine, sine):
    pieces, count, _ = rows.shape
    depth = own_panel.shape[1]
    total = pieces * count
    return pl.pallas_call(
        score_kernel,
        out_shape=jax.ShapeDtypeStruct((pieces, count, SH, depth), jnp.bfloat16),
        in_specs=[
            pl.BlockSpec(memory_space=pltpu.SMEM),
            pl.BlockSpec(memory_space=pltpu.VMEM),
            pl.BlockSpec(memory_space=pl.ANY),
            pl.BlockSpec(memory_space=pl.ANY),
            pl.BlockSpec(memory_space=pltpu.VMEM),
            pl.BlockSpec(memory_space=pltpu.VMEM),
        ],
        out_specs=pl.BlockSpec(memory_space=pltpu.VMEM),
        scratch_shapes=[
            pltpu.VMEM((total * HALVES, LANES), jnp.float32),
            pltpu.VMEM((TILE * SH, 2 * KF), jnp.bfloat16),
            pltpu.VMEM((TILE * SH, depth), jnp.float32),
            pltpu.VMEM((total, LANES), jnp.float32),
            pltpu.SMEM((total, LANES), jnp.float32),
            pltpu.SMEM((2, total + TILE), jnp.int32),
            pltpu.VMEM((2, 2 * KF, depth), jnp.bfloat16),
            pltpu.SemaphoreType.DMA,
            pltpu.SemaphoreType.DMA((2,)),
        ],
        compiler_params=pltpu.CompilerParams(vmem_limit_bytes=24 * 1024 * 1024),
        cost_estimate=pl.CostEstimate(
            flops=total * SH * depth * 4 * KF, bytes_accessed=16 << 20, transcendentals=0
        ),
        name="score",
    )(me, rows, own_panel, other_panel, cosine, sine)


def weigh_kernel(places, first, me_ref, *refs):
    parts, (weights_ref, log_ref) = refs[:places], refs[-2:]
    group, _, depth = parts[0].shape
    step = pl.program_id(0)

    @pl.when(step == 0)
    def _():
        log_ref[...] = refs[places + 1][...] if first else jnp.zeros(log_ref.shape, jnp.float32)

    lane = lax.broadcasted_iota(jnp.int32, log_ref.shape, 1)
    logs = log_ref[...]
    for g in range(group):
        total = sum(part[g].astype(jnp.float32) for part in parts)
        mean = jnp.sum(total, keepdims=True) / (SH * J)
        scale = 1.0 / mean
        for s in range(places):
            at = pl.multiple_of((me_ref[2] ^ s) * depth, depth)
            weights_ref[g, :, pl.ds(at, depth)] = parts[s][g].astype(jnp.float32) * scale
        logs = jnp.where(lane == first + step * group + g, jnp.log(mean), logs)
    log_ref[...] = logs


def weigh(me, parts, first, rows, before):
    places = len(parts)
    count, _, depth = parts[0].shape
    group = min(GROUP, count)
    logs = pl.BlockSpec((1, rows), lambda i: (0, 0))
    return pl.pallas_call(
        functools.partial(weigh_kernel, places, first),
        grid=(count // group,),
        out_shape=(
            jax.ShapeDtypeStruct((rows, SH, J), jnp.float32),
            jax.ShapeDtypeStruct((1, rows), jnp.float32),
        ),
        in_specs=[pl.BlockSpec(memory_space=pltpu.SMEM)]
        + [pl.BlockSpec((group, SH, depth), lambda i: (i, 0, 0))] * places
        + [pl.BlockSpec(memory_space=pl.ANY), logs][:len(before)],
        out_specs=(pl.BlockSpec((group, SH, J), lambda i: (first // group + i, 0, 0)), logs),
        input_output_aliases={places + 1: 0} if before else {},
        compiler_params=pltpu.CompilerParams(vmem_limit_bytes=16 * 1024 * 1024),
        name="weigh",
    )(me, *parts, *before)


def per_device(particles, classes, windows, pose_lists, inverse_noise, projections):
    owners = lax.axis_size("cls")
    places = lax.axis_size("proj")
    pairs = owners // 2
    label, place = lax.axis_index("cls"), lax.axis_index("proj")
    own_x = label // 2
    depth = projections.shape[1]
    me = jnp.stack([label, place * (depth // BLOCK), place]).astype(jnp.int32)

    def along_x(value, by):
        return lax.ppermute(value, "cls", [(i, i ^ (2 * by)) for i in range(owners)])

    def along_z(value, by):
        return lax.ppermute(value, "proj", [(i, i ^ by) for i in range(places)])

    chunks = pack(particles, classes, windows, pose_lists, inverse_noise)
    pieces = [[mine] + [along_z(mine, s) for s in range(1, places)] for mine in chunks]
    other_panel = lax.ppermute(projections[0], "cls", [(i, i ^ 1) for i in range(owners)])
    panels = turn(projections[0], other_panel)
    panels, pieces[1] = lax.optimization_barrier((panels, pieces[1]))
    columns = [jnp.stack(piece) for piece in pieces]
    far = [[along_x(column, f) for f in range(1, pairs)] for column in columns]
    far[0], columns[1:] = lax.optimization_barrier((far[0], columns[1:]))
    far_terms = []
    for group in far:
        terms = [score(me, rows, *panels) for rows in group]
        far_terms.append([along_x(t, f + 1) for f, t in enumerate(terms)])
    done, parts = (), None
    for j, column in enumerate(columns):
        column, terms = lax.optimization_barrier((column, terms))
        merged = score(me, column, *panels)
        owner_x = column[:, :, 2 * KF].astype(jnp.int32) // 2
        if j:
            far_terms[j], parts[1] = lax.optimization_barrier((far_terms[j], parts[1]))
            done = weigh(me, parts, (j - 1) * column.shape[1], particles.shape[0], done)
        for f in range(1, pairs):
            there = owner_x == (own_x ^ f)
            merged = jnp.where(there[:, :, None, None], far_terms[j][f - 1], merged)
        terms = merged
        parts = [merged[0]] + [along_z(merged[s], s) for s in range(1, places)]
    done = weigh(me, parts, (CHUNKS - 1) * column.shape[1], particles.shape[0], done)
    return done[0], done[1].reshape(-1)


def solution(mesh):
    placed = (
        P(("groups", "cls", "proj"), None),
        P(("groups", "cls", "proj"), None),
        P(("groups", "cls", "proj"), None),
        P(("groups", "cls", "proj"), None),
        P(("groups", "cls", "proj")),
        P("cls", "proj", None),
    )
    return jax.shard_map(
        per_device,
        mesh=mesh,
        in_specs=placed,
        out_specs=(P(("groups", "cls", "proj"), None, None), P(("groups", "cls", "proj"))),
        check_vma=False,
    )
```
